32 devices in a mesh: group: 2 (over y), dp: 8 (over z, x), tensor: 2 (over core).
Axes of the slice: x: 2, y: 2, z: 4, core: 2. Of those that a mesh axis runs over, the one named last changes fastest.
Arguments:
- hidden_states: bfloat16 [1, 16, 128, 8192], P(None, ('group', 'dp'), None, 'tensor'), parts along dimension 1, may hold values from -600 to 600
- up_grads: bfloat16 [1, 16, 128, 28672], P(None, ('group', 'dp'), None, 'tensor'), parts along dimension 1, may hold values from -6 to 6
- gains: bfloat16 [1, 8192], P(None, 'tensor'), may hold values from 0.25 to 1.75
- in_bases: bfloat16 [1, 8192, 64], P(None, ('tensor', 'dp')), may hold values from -0.0625 to 0.0625
- out_bases: bfloat16 [1, 28672, 64], P(None, ('tensor', 'dp')), may hold values from -0.03125 to 0.03125
- lengths: int32 [16], P(('group', 'dp')), parts along dimension 0, may hold values from 16 to 128, as said below
- queries: bfloat16 [32, 1, 4096], P(('group', 'dp')), parts along dimension 0, may hold values from -0.09375 to 0.09375
- query_ids: int32 [32], P('group'), parts along dimension 0, may hold values from 0 to 15, each once
Outputs:
- example_grads: bfloat16 [16, 1, 4096], P(('group', 'dp')), parts along dimension 0
- scores: float32 [16, 16], P(('group', 'dp')), parts along dimension 0
The draws below stay inside these ranges and needn't reach their ends.
There are 2 independent parts, one for each index of `group`. The reference program is written for one: setup_inputs(seed, part) draws one part's arguments, and reference() takes and returns one part's arrays. A program takes and returns all parts, laid end to end along the dimension named above; an argument that names none is the same for every part. Nothing has to cross between parts.
Inputs may be any that keep to these rules, and one draw needn't show every extreme that they name: lengths[e] counts the leading valid tokens of example e; some example of every draw has all 128.
All inputs are finite; a program needn't handle non-finite values.
Results may differ from the reference program's by a relative error of at most 0.012.
Values may be sent and summed in bfloat16 or wider, within the bound.
A program may use at most 64 MiB of HBM per device.

```python
import math
import jax
import jax.numpy as jnp
from jax import lax

D = 8192
FF = 28672
RANK = 64
LAYERS = 1
SEQ = 128
EXAMPLES = 8
QUERIES = 16


def draw_hidden_states(key, part):
    key = jax.random.fold_in(key, 11)
    key_base, key_rows, key_cols = jax.random.split(key, 3)
    shape = (LAYERS, EXAMPLES, SEQ, D)
    ramp = 1.0 + 2.0 * jnp.arange(D, dtype=jnp.float32) / D
    cols = jnp.exp(jax.random.uniform(key_cols, (LAYERS, 1, 1, D), jnp.float32) * math.log(3.0)) * ramp
    base = jnp.clip(jax.random.normal(key_base, shape, jnp.float32), -6.0, 6.0)
    rows = jnp.exp(jax.random.uniform(key_rows, (LAYERS, EXAMPLES, SEQ, 1), jnp.float32) * math.log(10.0))
    return (base * rows * cols).astype(jnp.bfloat16)


def draw_lengths(key, part):
    key = jax.random.fold_in(key, 5)
    key_len, key_pick = jax.random.split(key)
    values = jax.random.randint(key_len, (EXAMPLES,), SEQ // 8, SEQ + 1, jnp.int32)
    chosen = jax.random.randint(key_pick, (), 0, EXAMPLES, jnp.int32)
    return jnp.where(jnp.arange(EXAMPLES, dtype=jnp.int32) == chosen, SEQ, values).astype(jnp.int32)


def steps_of(own_key, extent, pieces, least, high):
    factor_of = 1.0
    for dim, shards_of in pieces:
        steps = jax.random.uniform(jax.random.fold_in(jax.random.fold_in(own_key, 6), dim), (shards_of,), jnp.float32, least / len(pieces), high / len(pieces))
        factor_of = factor_of * jnp.repeat(jnp.exp(steps), extent[dim] // shards_of).reshape((-1,) + (1,) * (len(extent) - 1 - dim))
    return factor_of


def gaussian(own_key, extent, scale, bound, pieces=(), held_as=jnp.bfloat16):
    entries = jax.random.normal(own_key, extent, jnp.float32) * scale
    if len(pieces) > 0:
        entries = steps_of(own_key, extent, pieces, -0.22, 0.18) * entries
    return jnp.clip(entries, min=-bound, max=bound).astype(held_as)


def setup_inputs(seed: int = 0, part: int = 0) -> dict:
    splits = jax.random.split(jax.random.key(seed), 9)
    part_splits = jax.random.split(jax.random.fold_in(splits[8], part), 9)
    hidden_states = draw_hidden_states(jax.random.fold_in(jax.random.fold_in(splits[8], part), 71), part)
    up_grads = gaussian(part_splits[1], (LAYERS, EXAMPLES, SEQ, FF), 1.0, 6.0, ((1, 8), (3, 2)))
    gains = jnp.clip(1.0 + 0.15 * jax.random.normal(splits[2], (LAYERS, D), jnp.float32), 0.25, 1.75).astype(jnp.bfloat16)
    in_bases = gaussian(splits[3], (LAYERS, D, RANK), D ** -0.5, 0.0625, ((1, 16),))
    out_bases = gaussian(splits[4], (LAYERS, FF, RANK), FF ** -0.5, 0.03125, ((1, 16),))
    lengths = draw_lengths(jax.random.fold_in(jax.random.fold_in(splits[8], part), 71), part)
    queries = gaussian(part_splits[6], (QUERIES, LAYERS, RANK * RANK), (LAYERS * RANK * RANK) ** -0.5, 0.09375, ((0, 8),))
    query_ids = jax.random.permutation(part_splits[7], QUERIES).astype(jnp.int32)
    return {"hidden_states": hidden_states, "up_grads": up_grads, "gains": gains, "in_bases": in_bases, "out_bases": out_bases, "lengths": lengths, "queries": queries, "query_ids": query_ids}


EPSILON = 1e-05

def reference(hidden_states, up_grads, gains, in_bases, out_bases, lengths, queries, query_ids):
    num_examples = hidden_states.shape[1]
    seq_len = hidden_states.shape[2]
    positions = jnp.arange(seq_len, dtype=jnp.int32)
    valid_mask = positions[None, :] < lengths[:, None]
    per_layer = []
    for layer_index in range(LAYERS):
        states = hidden_states[layer_index].astype(jnp.float32)
        inverse = lax.rsqrt(lax.optimization_barrier(jnp.sum(states * states, axis=-1)) / D + EPSILON)
        scaled = (states * gains[layer_index].astype(jnp.float32)[None, None, :]).astype(jnp.bfloat16)
        grad_rows = jnp.where(valid_mask[:, :, None], up_grads[layer_index], jnp.zeros((), jnp.bfloat16))
        proj_in = jnp.dot(scaled.reshape(-1, D), in_bases[layer_index], preferred_element_type=jnp.float32)
        proj_in = proj_in * inverse.reshape(-1, 1)
        proj_out = jnp.dot(grad_rows.reshape(-1, FF), out_bases[layer_index], preferred_element_type=jnp.float32)
        kronecker = jnp.einsum('esi,esj->eij', proj_in.reshape(num_examples, seq_len, RANK), proj_out.reshape(num_examples, seq_len, RANK))
        per_layer.append((kronecker * seq_len ** (-0.5)).reshape(num_examples, RANK * RANK))
    example_grads = jnp.stack(per_layer, axis=1).astype(jnp.bfloat16)
    all_scores = jnp.dot(example_grads.reshape(num_examples, -1), queries.reshape(queries.shape[0], -1).T, preferred_element_type=jnp.float32)
    scores = jnp.take(all_scores, query_ids, axis=1)
    return (example_grads, scores)
```

```python
import functools
import math

import jax
import jax.numpy as jnp
from jax import lax
from jax.experimental import pallas as pl
from jax.experimental.pallas import tpu as pltpu
from jax.sharding import PartitionSpec as P

EPSILON = 1e-05


def gathered_local(hidden_states, up_grads, gains, in_bases, out_bases, lengths, queries, query_ids):
    layer_count, example_count, seq_len, width_local = hidden_states.shape
    hidden_local = up_grads.shape[3]
    rank_size = in_bases.shape[2]
    states = hidden_states.astype(jnp.float32)
    squares = jnp.sum(states * states, axis=3)
    power = lax.psum(squares, "tensor")
    scaled = (states * gains.astype(jnp.float32)[:, None, None, :]).astype(jnp.bfloat16)
    positions = jnp.arange(seq_len, dtype=jnp.int32)
    valid_mask = positions[None, :] < lengths[:, None]
    grad_rows = jnp.where(valid_mask[None, :, :, None], up_grads, jnp.zeros((), jnp.bfloat16))
    flat_in = scaled.reshape(layer_count, example_count * seq_len, width_local)
    flat_out = grad_rows.reshape(layer_count, example_count * seq_len, hidden_local)
    shard_in = in_bases.shape[1]
    shard_out = out_bases.shape[1]
    blocks = math.gcd(shard_in, shard_out)
    per_in = shard_in // blocks
    per_out = shard_out // blocks
    grouped_in = in_bases.reshape(layer_count, blocks, per_in * rank_size)
    grouped_out = out_bases.reshape(layer_count, blocks, per_out * rank_size)
    pieces = (
        lax.all_gather(grouped_in, "dp", axis=1, tiled=True),
        lax.all_gather(grouped_out, "dp", axis=1, tiled=True),
    )
    block_count = pieces[0].shape[1]
    rows_in = pieces[0].reshape(layer_count, block_count * per_in, rank_size)
    rows_out = pieces[1].reshape(layer_count, block_count * per_out, rank_size)
    new_in = jnp.einsum("ltd,ldr->ltr", flat_in, rows_in, preferred_element_type=jnp.float32)
    new_out = jnp.einsum("ltd,ldr->ltr", flat_out, rows_out, preferred_element_type=jnp.float32)
    proj_in = new_in
    proj_out = new_out
    proj_in, proj_out = lax.psum((proj_in, proj_out), "tensor")
    full_width = width_local * lax.axis_size("tensor")
    inverse = lax.rsqrt(power / full_width + EPSILON)
    proj_in = proj_in * inverse.reshape(layer_count, example_count * seq_len)[:, :, None]
    kronecker = jnp.einsum(
        "lesi,lesj->elij",
        proj_in.reshape(layer_count, example_count, seq_len, rank_size),
        proj_out.reshape(layer_count, example_count, seq_len, rank_size),
    )
    example_grads = (
        (kronecker * seq_len ** (-0.5))
        .reshape(example_count, layer_count, rank_size * rank_size)
        .astype(jnp.bfloat16)
    )
    flat_grads = example_grads.reshape(example_count, layer_count * rank_size * rank_size)
    in_piece = lax.all_gather(queries, "dp", axis=0, tiled=True)
    all_scores = jnp.einsum(
        "ek,qk->eq",
        flat_grads,
        in_piece.reshape(in_piece.shape[0], -1),
        preferred_element_type=jnp.float32,
    )
    scores = jnp.take(all_scores, query_ids, axis=1)
    return (example_grads, scores)


def remote(src, dst, send_sem, recv_sem, where):
    return pltpu.make_async_remote_copy(
        src_ref=src,
        dst_ref=dst,
        send_sem=send_sem,
        recv_sem=recv_sem,
        device_id=where,
        device_id_type=pl.DeviceIdType.MESH,
    )


def kernel(
    planes,
    hidden_ref,
    grads_ref,
    gains_ref,
    in_ref,
    out_ref,
    lengths_ref,
    queries_ref,
    ids_ref,
    flat_ref,
    scores_ref,
    bases,
    hidden,
    scaled,
    grads,
    sum_in,
    sum_out,
    power,
    peer_power,
    mine,
    theirs,
    wide,
    all_queries,
    local_sem,
    z_send,
    z_recv,
    x_send,
    x_recv,
    y_send,
    y_recv,
    x2_send,
    x2_recv,
    y2_send,
    y2_recv,
    q_send,
    q_recv,
    t_send,
    t_recv,
):
    group, dp, tensor = lax.axis_index("group"), lax.axis_index("dp"), lax.axis_index("tensor")
    z, x, y = dp // 2, dp % 2, group
    count = 2 * planes
    x_peer, y_peer, t_peer = {"dp": 2 * z + 1 - x}, {"group": 1 - y}, {"tensor": 1 - tensor}
    rank, wide_in, wide_out = in_ref.shape[0], in_ref.shape[1], out_ref.shape[1]
    half, quarter = rank // 2, rank // 4
    seq = hidden.shape[0]

    own_in = pltpu.make_async_copy(in_ref, bases.at[dp, :, pl.ds(0, wide_in)], local_sem.at[0])
    own_out = pltpu.make_async_copy(out_ref, bases.at[dp, :, pl.ds(wide_in, wide_out)], local_sem.at[1])
    own_hidden = pltpu.make_async_copy(hidden_ref, hidden, local_sem.at[2])
    own_grads = pltpu.make_async_copy(grads_ref, grads, local_sem.at[3])
    own_queries = pltpu.make_async_copy(queries_ref, all_queries.at[dp], local_sem.at[4])
    own_in.start()
    own_out.start()
    own_queries.start()
    own_hidden.start()
    own_grads.start()

    barrier = pltpu.get_barrier_semaphore()
    for step in range(1, count):
        pl.semaphore_signal(barrier, inc=1, device_id={"dp": (dp + step) % count}, device_id_type=pl.DeviceIdType.MESH)
    pl.semaphore_signal(barrier, inc=1, device_id=y_peer, device_id_type=pl.DeviceIdType.MESH)
    pl.semaphore_signal(barrier, inc=1, device_id=t_peer, device_id_type=pl.DeviceIdType.MESH)
    own_in.wait()
    own_out.wait()
    own_queries.wait()
    pl.semaphore_wait(barrier, count + 1)

    def rows(start, size):
        return pl.ds(pl.multiple_of(start, quarter), size)

    def part(plane, column, side):
        return bases.at[2 * plane + column, rows(half * side, half), :]

    def fourth(plane, column, side, which):
        return bases.at[2 * plane + column, rows(half * side + quarter * which, quarter), :]

    def along_z(plane, up):
        there = {"dp": dp + 2} if up else {"dp": dp - 2}
        ref = part(plane, x, y)
        return remote(ref, ref, z_send.at[int(up), plane], z_recv.at[plane], there)

    def over_x(plane, column):
        ref = part(plane, column, y)
        return remote(ref, ref, x_send.at[plane], x_recv.at[plane], x_peer)

    def over_y(plane, column, side):
        ref = part(plane, column, side)
        return remote(ref, ref, y_send.at[plane], y_recv.at[plane], y_peer)

    def second_x(plane, column, side):
        ref = fourth(plane, column, side, 0)
        return remote(ref, ref, x2_send.at[plane], x2_recv.at[plane], x_peer)

    def second_y(plane, column, side):
        ref = fourth(plane, column, side, 1)
        return remote(ref, ref, y2_send.at[plane], y2_recv.at[plane], y_peer)

    def to_query(step):
        there = (dp + step) % count
        return remote(all_queries.at[dp], all_queries.at[dp], q_send.at[step - 1], q_recv.at[dp], {"dp": there})

    def multiply(unit):
        at_in = pl.ds(pl.multiple_of(unit * wide_in, wide_in), wide_in)
        at_out = pl.ds(pl.multiple_of(unit * wide_out, wide_out), wide_out)
        contract = (((1,), (1,)), ((), ()))
        sum_in[...] += lax.dot_general(
            scaled[:, at_in], bases[unit, :, :wide_in], contract, preferred_element_type=jnp.float32
        )
        sum_out[...] += lax.dot_general(
            grads[:, at_out], bases[unit, :, wide_in:], contract, preferred_element_type=jnp.float32
        )

    remote_planes = [(step, up) for step in range(1, planes) for up in (True, False)]

    def place(step, up):
        plane = z - step if up else z + step
        return plane, (plane >= 0) if up else (plane < planes)

    def onward(up):
        return (z < planes - 1) if up else (z > 0)

    @pl.when(onward(True))
    def _():
        along_z(z, True).start()

    @pl.when(onward(False))
    def _():
        along_z(z, False).start()

    over_x(z, x).start()

    own_hidden.wait()
    total = jnp.zeros((seq, 128), jnp.float32)
    for start in range(0, hidden.shape[1], 128):
        states = hidden[:, start : start + 128].astype(jnp.float32)
        total += states * states
        gain = gains_ref[:, start : start + 128].astype(jnp.float32)
        scaled[:, start : start + 128] = (states * gain).astype(jnp.bfloat16)
    power[...] = jnp.broadcast_to(jnp.sum(total, axis=1, keepdims=True), (seq, 128))
    send_power = remote(power, peer_power, t_send.at[0], t_recv.at[0], t_peer)
    send_power.start()
    sum_in[...] = jnp.zeros_like(sum_in)
    sum_out[...] = jnp.zeros_like(sum_out)
    own_grads.wait()
    multiply(dp)

    over_x(z, 1 - x).wait_recv()
    over_y(z, 1 - x, y).start()

    def first_hops(step, up):
        plane, there = place(step, up)

        @pl.when(there)
        def _():
            along_z(plane, up).wait_recv()
            if step < planes - 1:

                @pl.when(onward(up))
                def _():
                    along_z(plane, up).start()

            over_x(plane, x).start()
            over_y(plane, x, y).start()

    def second_hops(step, up):
        plane, there = place(step, up)

        @pl.when(there)
        def _():
            over_x(plane, 1 - x).wait_recv()
            second_y(plane, 1 - x, y).start()
            over_y(plane, x, 1 - y).wait_recv()
            second_x(plane, x, 1 - y).start()

    def finish(step, up):
        plane, there = place(step, up)

        @pl.when(there)
        def _():
            multiply(2 * plane + x)
            second_x(plane, 1 - x, 1 - y).wait_recv()
            second_y(plane, 1 - x, 1 - y).wait_recv()
            multiply(2 * plane + 1 - x)

    for step in range(1, planes):
        for up in (True, False):
            first_hops(step, up)
        if step == 1:
            for other in range(1, count):
                to_query(other).start()
            over_y(z, 1 - x, 1 - y).wait_recv()
            multiply(2 * z + 1 - x)
        else:
            for up in (True, False):
                finish(step - 1, up)
        for up in (True, False):
            second_hops(step, up)
    for up in (True, False):
        finish(planes - 1, up)

    mine[0] = sum_in[...]
    mine[1] = sum_out[...]
    send_sums = remote(mine, theirs, t_send.at[1], t_recv.at[1], t_peer)
    send_sums.start()
    send_power.wait_recv()
    mean = (power[...] + peer_power[...]) / (2 * hidden.shape[1])
    inverse = lax.rsqrt(mean + EPSILON)[:, :rank]
    valid = lax.broadcasted_iota(jnp.int32, (seq, rank), 0) < lengths_ref[0]
    for other in range(1, count):
        remote(
            all_queries.at[dp], all_queries.at[(dp + other) % count], q_send.at[other - 1], q_recv.at[(dp + other) % count], x_peer
        ).wait_recv()
    send_sums.wait_recv()
    proj_in = ((mine[0] + theirs[0]) * inverse).astype(jnp.bfloat16)
    proj_out = jnp.where(valid, mine[1] + theirs[1], 0.0).astype(jnp.bfloat16)
    wide[...] = lax.dot_general(
        proj_in,
        jnp.concatenate([proj_out, proj_out], axis=1),
        (((0,), (0,)), ((), ())),
        preferred_element_type=jnp.float32,
    )
    even = wide[pl.ds(0, half, stride=2), :]
    odd = wide[pl.ds(1, half, stride=2), :]
    lane = lax.broadcasted_iota(jnp.int32, (half, 2 * rank), 1)
    flat = (jnp.where(lane < rank, even, odd) * seq ** (-0.5)).astype(jnp.bfloat16)
    flat_ref[...] = flat
    flat = flat.astype(jnp.float32)
    per_device = all_queries.shape[1]
    score = jnp.zeros((count, per_device, 128), jnp.float32)
    for row in range(half):
        block = all_queries[:, :, row * 128 : (row + 1) * 128].astype(jnp.float32)
        score += block * flat[row : row + 1, :][None]
    score = jnp.sum(score, axis=2, keepdims=True)
    columns = ids_ref.shape[1]
    number = per_device * lax.broadcasted_iota(jnp.int32, (count, per_device, columns), 0) + lax.broadcasted_iota(
        jnp.int32, (count, per_device, columns), 1
    )
    picked = jnp.where(number == ids_ref[...][None], score, 0.0)
    scores_ref[...] = jnp.sum(jnp.sum(picked, axis=0), axis=0, keepdims=True)

    @pl.when(onward(True))
    def _():
        along_z(z, True).wait_send()

    @pl.when(onward(False))
    def _():
        along_z(z, False).wait_send()

    over_x(z, x).wait_send()
    over_y(z, 1 - x, y).wait_send()
    for step, up in remote_planes:
        plane, there = place(step, up)

        @pl.when(there)
        def _(step=step, up=up, plane=plane):
            if step < planes - 1:

                @pl.when(onward(up))
                def _():
                    along_z(plane, up).wait_send()

            over_x(plane, x).wait_send()
            over_y(plane, x, y).wait_send()
            second_y(plane, 1 - x, y).wait_send()
            second_x(plane, x, 1 - y).wait_send()

    for other in range(1, count):
        to_query(other).wait_send()
    send_power.wait_send()
    send_sums.wait_send()


def local(hidden_states, up_grads, gains, in_bases, out_bases, lengths, queries, query_ids):
    layer_count, example_count, seq, width = hidden_states.shape
    hidden_units = up_grads.shape[3]
    shard_in, rank = in_bases.shape[1:]
    shard_out = out_bases.shape[1]
    count = lax.axis_size("dp")
    fits = (
        (layer_count, example_count, rank, lax.axis_size("group"), lax.axis_size("tensor")) == (1, 1, 64, 2, 2)
        and count % 2 == 0
        and shard_in % 128 == 0
        and shard_out % 128 == 0
    )
    if not fits:
        return gathered_local(hidden_states, up_grads, gains, in_bases, out_bases, lengths, queries, query_ids)
    planes = count // 2
    anywhere, vmem = pl.BlockSpec(memory_space=pl.ANY), pl.BlockSpec(memory_space=pltpu.VMEM)
    pairs = pltpu.SemaphoreType.DMA((planes,))
    f32, bf16 = jnp.float32, jnp.bfloat16
    flat, scores = pl.pallas_call(
        functools.partial(kernel, planes),
        out_shape=(
            jax.ShapeDtypeStruct((rank // 2, 2 * rank), bf16),
            jax.ShapeDtypeStruct((1, query_ids.shape[0]), f32),
        ),
        in_specs=[anywhere, anywhere, vmem, anywhere, anywhere, pl.BlockSpec(memory_space=pltpu.SMEM), anywhere, vmem],
        out_specs=(vmem, vmem),
        scratch_shapes=[
            pltpu.VMEM((count, rank, shard_in + shard_out), bf16),
            pltpu.VMEM((seq, width), bf16),
            pltpu.VMEM((seq, width), bf16),
            pltpu.VMEM((seq, hidden_units), bf16),
            pltpu.VMEM((seq, rank), f32),
            pltpu.VMEM((seq, rank), f32),
            pltpu.VMEM((seq, 128), f32),
            pltpu.VMEM((seq, 128), f32),
            pltpu.VMEM((2, seq, rank), f32),
            pltpu.VMEM((2, seq, rank), f32),
            pltpu.VMEM((rank, 2 * rank), f32),
            pltpu.VMEM((count, queries.shape[0], rank * rank), bf16),
            pltpu.SemaphoreType.DMA((5,)),
            pltpu.SemaphoreType.DMA((2, planes)),
            pairs,
            pairs,
            pairs,
            pairs,
            pairs,
            pairs,
            pairs,
            pairs,
            pairs,
            pltpu.SemaphoreType.DMA((count - 1,)),
            pltpu.SemaphoreType.DMA((count,)),
            pltpu.SemaphoreType.DMA((2,)),
            pltpu.SemaphoreType.DMA((2,)),
        ],
        compiler_params=pltpu.CompilerParams(
            collective_id=0, has_side_effects=True, vmem_limit_bytes=48 * 1024 * 1024
        ),
    )(
        hidden_states.reshape(seq, width),
        up_grads.reshape(seq, hidden_units),
        gains,
        in_bases[0].T,
        out_bases[0].T,
        lengths,
        queries.reshape(queries.shape[0], -1),
        query_ids.reshape(1, -1),
    )
    return flat.reshape(1, 1, rank * rank), scores


def solution(mesh):
    placed = (
        P(None, ("group", "dp"), None, "tensor"),
        P(None, ("group", "dp"), None, "tensor"),
        P(None, "tensor"),
        P(None, ("tensor", "dp"), None),
        P(None, ("tensor", "dp"), None),
        P(("group", "dp")),
        P(("group", "dp"), None, None),
        P("group"),
    )
    return jax.shard_map(
        local,
        mesh=mesh,
        in_specs=placed,
        out_specs=(P(("group", "dp"), None, None), P(("group", "dp"), None)),
        check_vma=False,
    )
```

```python
import functools
import math

import jax
import jax.numpy as jnp
from jax import lax
from jax.experimental import pallas as pl
from jax.experimental.pallas import tpu as pltpu
from jax.sharding import PartitionSpec as P

EPSILON = 1e-05


def gathered_local(hidden_states, up_grads, gains, in_bases, out_bases, lengths, queries, query_ids):
    layer_count, example_count, seq_len, width_local = hidden_states.shape
    hidden_local = up_grads.shape[3]
    rank_size = in_bases.shape[2]
    states = hidden_states.astype(jnp.float32)
    squares = jnp.sum(states * states, axis=3)
    power = lax.psum(squares, "tensor")
    scaled = (states * gains.astype(jnp.float32)[:, None, None, :]).astype(jnp.bfloat16)
    positions = jnp.arange(seq_len, dtype=jnp.int32)
    valid_mask = positions[None, :] < lengths[:, None]
    grad_rows = jnp.where(valid_mask[None, :, :, None], up_grads, jnp.zeros((), jnp.bfloat16))
    flat_in = scaled.reshape(layer_count, example_count * seq_len, width_local)
    flat_out = grad_rows.reshape(layer_count, example_count * seq_len, hidden_local)
    shard_in = in_bases.shape[1]
    shard_out = out_bases.shape[1]
    blocks = math.gcd(shard_in, shard_out)
    per_in = shard_in // blocks
    per_out = shard_out // blocks
    grouped_in = in_bases.reshape(layer_count, blocks, per_in * rank_size)
    grouped_out = out_bases.reshape(layer_count, blocks, per_out * rank_size)
    pieces = (
        lax.all_gather(grouped_in, "dp", axis=1, tiled=True),
        lax.all_gather(grouped_out, "dp", axis=1, tiled=True),
    )
    block_count = pieces[0].shape[1]
    rows_in = pieces[0].reshape(layer_count, block_count * per_in, rank_size)
    rows_out = pieces[1].reshape(layer_count, block_count * per_out, rank_size)
    new_in = jnp.einsum("ltd,ldr->ltr", flat_in, rows_in, preferred_element_type=jnp.float32)
    new_out = jnp.einsum("ltd,ldr->ltr", flat_out, rows_out, preferred_element_type=jnp.float32)
    proj_in = new_in
    proj_out = new_out
    proj_in, proj_out = lax.psum((proj_in, proj_out), "tensor")
    full_width = width_local * lax.axis_size("tensor")
    inverse = lax.rsqrt(power / full_width + EPSILON)
    proj_in = proj_in * inverse.reshape(layer_count, example_count * seq_len)[:, :, None]
    kronecker = jnp.einsum(
        "lesi,lesj->elij",
        proj_in.reshape(layer_count, example_count, seq_len, rank_size),
        proj_out.reshape(layer_count, example_count, seq_len, rank_size),
    )
    example_grads = (
        (kronecker * seq_len ** (-0.5))
        .reshape(example_count, layer_count, rank_size * rank_size)
        .astype(jnp.bfloat16)
    )
    flat_grads = example_grads.reshape(example_count, layer_count * rank_size * rank_size)
    in_piece = lax.all_gather(queries, "dp", axis=0, tiled=True)
    all_scores = jnp.einsum(
        "ek,qk->eq",
        flat_grads,
        in_piece.reshape(in_piece.shape[0], -1),
        preferred_element_type=jnp.float32,
    )
    scores = jnp.take(all_scores, query_ids, axis=1)
    return (example_grads, scores)


def remote(src, dst, send_sem, recv_sem, where):
    return pltpu.make_async_remote_copy(
        src_ref=src,
        dst_ref=dst,
        send_sem=send_sem,
        recv_sem=recv_sem,
        device_id=where,
        device_id_type=pl.DeviceIdType.MESH,
    )


def kernel(
    planes,
    chunks,
    lag,
    late,
    hidden_ref,
    grads_ref,
    gains_hbm,
    in_ref,
    out_ref,
    lengths_hbm,
    queries_ref,
    ids_hbm,
    flat_ref,
    scores_ref,
    bases,
    hidden,
    scaled,
    grads,
    sum_in,
    sum_out,
    power,
    peer_power,
    mine,
    theirs,
    wide,
    all_queries,
    gains_ref,
    lengths_ref,
    ids_ref,
    local_sem,
    z_send,
    z_recv,
    x_send,
    x_recv,
    y_send,
    y_recv,
    x2_send,
    x2_recv,
    y2_send,
    y2_recv,
    q_send,
    q_recv,
    t_send,
    t_recv,
):
    group, dp, tensor = lax.axis_index("group"), lax.axis_index("dp"), lax.axis_index("tensor")
    z, x, y = dp // 2, dp % 2, group
    count = 2 * planes
    x_peer, y_peer, t_peer = {"dp": 2 * z + 1 - x}, {"group": 1 - y}, {"tensor": 1 - tensor}
    rank, wide_in, wide_out = in_ref.shape[0], in_ref.shape[1], out_ref.shape[1]
    half, quarter = rank // 2, rank // 4
    width = (wide_in + wide_out) // chunks
    seq = hidden.shape[0]

    own_in = pltpu.make_async_copy(in_ref, bases.at[dp, :, pl.ds(0, wide_in)], local_sem.at[0])
    own_out = pltpu.make_async_copy(out_ref, bases.at[dp, :, pl.ds(wide_in, wide_out)], local_sem.at[1])
    own_hidden = pltpu.make_async_copy(hidden_ref, hidden, local_sem.at[2])
    own_grads = pltpu.make_async_copy(grads_ref, grads, local_sem.at[3])
    own_queries = pltpu.make_async_copy(queries_ref, all_queries.at[dp], local_sem.at[4])
    own_gains = pltpu.make_async_copy(gains_hbm, gains_ref, local_sem.at[5])
    own_lengths = pltpu.make_async_copy(lengths_hbm, lengths_ref, local_sem.at[6])
    own_ids = pltpu.make_async_copy(ids_hbm, ids_ref, local_sem.at[7])
    own_in.start()
    own_out.start()
    own_gains.start()
    own_queries.start()
    own_lengths.start()
    own_ids.start()
    own_hidden.start()
    own_grads.start()

    barrier = pltpu.get_barrier_semaphore()
    for step in range(1, count):
        pl.semaphore_signal(barrier, inc=1, device_id={"dp": (dp + step) % count}, device_id_type=pl.DeviceIdType.MESH)
    pl.semaphore_signal(barrier, inc=1, device_id=y_peer, device_id_type=pl.DeviceIdType.MESH)
    pl.semaphore_signal(barrier, inc=1, device_id=t_peer, device_id_type=pl.DeviceIdType.MESH)
    own_in.wait()
    own_out.wait()
    own_queries.wait()
    pl.semaphore_wait(barrier, count + 1)

    def rows(start, size):
        return pl.ds(pl.multiple_of(start, quarter), size)

    def columns(chunk):
        return pl.ds(chunk * width, width)

    def part(plane, column, side, chunk):
        return bases.at[2 * plane + column, rows(half * side, half), columns(chunk)]

    def fourth(plane, column, side, which, chunk):
        return bases.at[2 * plane + column, rows(half * side + quarter * which, quarter), columns(chunk)]

    def along_z(plane, up, c):
        there = {"dp": dp + 2} if up else {"dp": dp - 2}
        ref = part(plane, x, y, c)
        return remote(ref, ref, z_send.at[int(up), plane, c], z_recv.at[plane, c], there)

    def over_x(plane, column, c):
        ref = part(plane, column, y, c)
        return remote(ref, ref, x_send.at[plane, c], x_recv.at[plane, c], x_peer)

    def over_y(plane, column, side, c):
        ref = part(plane, column, side, c)
        return remote(ref, ref, y_send.at[plane, c], y_recv.at[plane, c], y_peer)

    def second_x(plane, column, side, c):
        ref = fourth(plane, column, side, 0, c)
        return remote(ref, ref, x2_send.at[plane, c], x2_recv.at[plane, c], x_peer)

    def second_y(plane, column, side, c):
        ref = fourth(plane, column, side, 1, c)
        return remote(ref, ref, y2_send.at[plane, c], y2_recv.at[plane, c], y_peer)

    def to_query(step):
        there = (dp + step) % count
        return remote(all_queries.at[dp], all_queries.at[dp], q_send.at[step - 1], q_recv.at[dp], {"dp": there})

    def multiply(unit, chunk):
        contract = (((1,), (1,)), ((), ()))
        low, high = chunk * width, (chunk + 1) * width
        for into, values, start, size in ((sum_in, scaled, 0, wide_in), (sum_out, grads, wide_in, wide_out)):
            first, last = max(low, start), min(high, start + size)
            if first < last:
                at = pl.ds(pl.multiple_of(unit * size + (first - start), 128), last - first)
                into[...] += lax.dot_general(
                    values[:, at], bases[unit, :, first:last], contract, preferred_element_type=jnp.float32
                )

    remote_planes = [(step, up) for step in range(1, planes) for up in (True, False)]

    def place(step, up):
        plane = z - step if up else z + step
        return plane, (plane >= 0) if up else (plane < planes)

    def onward(up):
        return (z < planes - 1) if up else (z > 0)

    for c in range(chunks):

        @pl.when(onward(True))
        def _(c=c):
            along_z(z, True, c).start()

        @pl.when(onward(False))
        def _(c=c):
            along_z(z, False, c).start()

        over_x(z, x, c).start()

    own_gains.wait()
    own_hidden.wait()
    total = jnp.zeros((seq, 128), jnp.float32)
    for start in range(0, hidden.shape[1], 128):
        states = hidden[:, start : start + 128].astype(jnp.float32)
        total += states * states
        gain = gains_ref[:, start : start + 128].astype(jnp.float32)
        scaled[:, start : start + 128] = (states * gain).astype(jnp.bfloat16)
    power[...] = jnp.broadcast_to(jnp.sum(total, axis=1, keepdims=True), (seq, 128))
    send_power = remote(power, peer_power, t_send.at[0], t_recv.at[0], t_peer)
    send_power.start()
    sum_in[...] = jnp.zeros_like(sum_in)
    sum_out[...] = jnp.zeros_like(sum_out)
    own_grads.wait()
    for c in range(chunks):
        multiply(dp, c)

    def first_hop(step, up, c):
        plane, there = place(step, up)

        @pl.when(there)
        def _():
            along_z(plane, up, c).wait_recv()
            if step < planes - 1:

                @pl.when(onward(up))
                def _():
                    along_z(plane, up, c).start()

            over_x(plane, x, c).start()
            over_y(plane, x, y, c).start()

    def second_hop(step, up, c):
        plane, there = place(step, up)

        @pl.when(there)
        def _():
            over_x(plane, 1 - x, c).wait_recv()
            second_y(plane, 1 - x, y, c).start()
            over_y(plane, x, 1 - y, c).wait_recv()
            second_x(plane, x, 1 - y, c).start()
            multiply(2 * plane + x, c)

    def finish(step, up, c):
        plane, there = place(step, up)

        @pl.when(there)
        def _():
            second_x(plane, 1 - x, 1 - y, c).wait_recv()
            second_y(plane, 1 - x, 1 - y, c).wait_recv()
            multiply(2 * plane + 1 - x, c)

    slots = (planes - 1) * chunks
    for slot in range(slots + lag + late):
        if slot < slots:
            for up in (True, False):
                first_hop(slot // chunks + 1, up, slot % chunks)
        if slot == chunks:
            for other in range(1, count):
                to_query(other).start()
        again = slot - lag
        if -chunks <= again < 0:
            over_x(z, 1 - x, again + chunks).wait_recv()
            over_y(z, 1 - x, y, again + chunks).start()
        elif 0 <= again < slots:
            for up in (True, False):
                second_hop(again // chunks + 1, up, again % chunks)
        last = slot - lag - late
        if -chunks <= last < 0:
            over_y(z, 1 - x, 1 - y, last + chunks).wait_recv()
            multiply(2 * z + 1 - x, last + chunks)
        elif 0 <= last < slots:
            for up in (True, False):
                finish(last // chunks + 1, up, last % chunks)

    mine[0] = sum_in[...]
    mine[1] = sum_out[...]
    send_sums = remote(mine, theirs, t_send.at[1], t_recv.at[1], t_peer)
    send_sums.start()
    send_power.wait_recv()
    mean = (power[...] + peer_power[...]) / (2 * hidden.shape[1])
    inverse = lax.rsqrt(mean + EPSILON)[:, :rank]
    own_lengths.wait()
    own_ids.wait()
    valid = lax.broadcasted_iota(jnp.int32, (seq, rank), 0) < lengths_ref[0]
    for other in range(1, count):
        remote(
            all_queries.at[dp], all_queries.at[(dp + other) % count], q_send.at[other - 1], q_recv.at[(dp + other) % count], x_peer
        ).wait_recv()
    send_sums.wait_recv()
    proj_in = ((mine[0] + theirs[0]) * inverse).astype(jnp.bfloat16)
    proj_out = jnp.where(valid, mine[1] + theirs[1], 0.0).astype(jnp.bfloat16)
    wide[...] = lax.dot_general(
        proj_in,
        jnp.concatenate([proj_out, proj_out], axis=1),
        (((0,), (0,)), ((), ())),
        preferred_element_type=jnp.float32,
    )
    even = wide[pl.ds(0, half, stride=2), :]
    odd = wide[pl.ds(1, half, stride=2), :]
    lane = lax.broadcasted_iota(jnp.int32, (half, 2 * rank), 1)
    flat = (jnp.where(lane < rank, even, odd) * seq ** (-0.5)).astype(jnp.bfloat16)
    flat_ref[...] = flat
    flat = flat.astype(jnp.float32)
    per_device = all_queries.shape[1]
    score = jnp.zeros((count, per_device, 128), jnp.float32)
    for row in range(half):
        block = all_queries[:, :, row * 128 : (row + 1) * 128].astype(jnp.float32)
        score += block * flat[row : row + 1, :][None]
    score = jnp.sum(score, axis=2, keepdims=True)
    places = ids_ref.shape[1]
    number = per_device * lax.broadcasted_iota(jnp.int32, (count, per_device, places), 0) + lax.broadcasted_iota(
        jnp.int32, (count, per_device, places), 1
    )
    picked = jnp.where(number == ids_ref[...][None], score, 0.0)
    scores_ref[...] = jnp.sum(jnp.sum(picked, axis=0), axis=0, keepdims=True)

    for c in range(chunks):

        @pl.when(onward(True))
        def _(c=c):
            along_z(z, True, c).wait_send()

        @pl.when(onward(False))
        def _(c=c):
            along_z(z, False, c).wait_send()

        over_x(z, x, c).wait_send()
        over_y(z, 1 - x, y, c).wait_send()
        for step, up in remote_planes:
            plane, there = place(step, up)

            @pl.when(there)
            def _(step=step, up=up, plane=plane, c=c):
                if step < planes - 1:

                    @pl.when(onward(up))
                    def _():
                        along_z(plane, up, c).wait_send()

                over_x(plane, x, c).wait_send()
                over_y(plane, x, y, c).wait_send()
                second_y(plane, 1 - x, y, c).wait_send()
                second_x(plane, x, 1 - y, c).wait_send()

    for other in range(1, count):
        to_query(other).wait_send()
    send_power.wait_send()
    send_sums.wait_send()


def local(hidden_states, up_grads, gains, in_bases, out_bases, lengths, queries, query_ids):
    layer_count, example_count, seq, width = hidden_states.shape
    hidden_units = up_grads.shape[3]
    shard_in, rank = in_bases.shape[1:]
    shard_out = out_bases.shape[1]
    count = lax.axis_size("dp")
    fits = (
        (layer_count, example_count, rank, lax.axis_size("group"), lax.axis_size("tensor")) == (1, 1, 64, 2, 2)
        and count % 2 == 0
        and shard_in % 128 == 0
        and shard_out % 128 == 0
    )
    if not fits:
        return gathered_local(hidden_states, up_grads, gains, in_bases, out_bases, lengths, queries, query_ids)
    planes = count // 2
    tiles = (shard_in + shard_out) // 128
    chunks = 3 if tiles % 3 == 0 else 1
    hbm, vmem = pl.BlockSpec(memory_space=pltpu.HBM), pl.BlockSpec(memory_space=pltpu.VMEM)
    pairs = pltpu.SemaphoreType.DMA((planes, chunks))
    f32, bf16 = jnp.float32, jnp.bfloat16
    flat, scores = pl.pallas_call(
        functools.partial(kernel, planes, chunks, chunks + 1, chunks),
        out_shape=(
            jax.ShapeDtypeStruct((rank // 2, 2 * rank), bf16),
            jax.ShapeDtypeStruct((1, query_ids.shape[0]), f32),
        ),
        in_specs=[hbm] * 8,
        out_specs=(vmem, vmem),
        scratch_shapes=[
            pltpu.VMEM((count, rank, shard_in + shard_out), bf16),
            pltpu.VMEM((seq, width), bf16),
            pltpu.VMEM((seq, width), bf16),
            pltpu.VMEM((seq, hidden_units), bf16),
            pltpu.VMEM((seq, rank), f32),
            pltpu.VMEM((seq, rank), f32),
            pltpu.VMEM((seq, 128), f32),
            pltpu.VMEM((seq, 128), f32),
            pltpu.VMEM((2, seq, rank), f32),
            pltpu.VMEM((2, seq, rank), f32),
            pltpu.VMEM((rank, 2 * rank), f32),
            pltpu.VMEM((count, queries.shape[0], rank * rank), bf16),
            pltpu.VMEM((1, width), bf16),
            pltpu.SMEM(lengths.shape, jnp.int32),
            pltpu.VMEM((1, query_ids.shape[0]), jnp.int32),
            pltpu.SemaphoreType.DMA((8,)),
            pltpu.SemaphoreType.DMA((2, planes, chunks)),
            pairs,
            pairs,
            pairs,
            pairs,
            pairs,
            pairs,
            pairs,
            pairs,
            pairs,
            pltpu.SemaphoreType.DMA((count - 1,)),
            pltpu.SemaphoreType.DMA((count,)),
            pltpu.SemaphoreType.DMA((2,)),
            pltpu.SemaphoreType.DMA((2,)),
        ],
        compiler_params=pltpu.CompilerParams(
            collective_id=0, has_side_effects=True, vmem_limit_bytes=64 * 1024 * 1024
        ),
    )(
        hidden_states.reshape(seq, width),
        up_grads.reshape(seq, hidden_units),
        gains,
        in_bases[0].T,
        out_bases[0].T,
        lengths,
        queries.reshape(queries.shape[0], -1),
        query_ids.reshape(1, -1),
    )
    return flat.reshape(1, 1, rank * rank), scores


def solution(mesh):
    placed = (
        P(None, ("group", "dp"), None, "tensor"),
        P(None, ("group", "dp"), None, "tensor"),
        P(None, "tensor"),
        P(None, ("tensor", "dp"), None),
        P(None, ("tensor", "dp"), None),
        P(("group", "dp")),
        P(("group", "dp"), None, None),
        P("group"),
    )
    return jax.shard_map(
        local,
        mesh=mesh,
        in_specs=placed,
        out_specs=(P(("group", "dp"), None, None), P(("group", "dp"), None)),
        check_vma=False,
    )
```

```python
import functools
import math

import jax
import jax.numpy as jnp
from jax import lax
from jax.experimental import pallas as pl
from jax.experimental.pallas import tpu as pltpu
from jax.sharding import PartitionSpec as P

EPSILON = 1e-05


def gathered_local(hidden_states, up_grads, gains, in_bases, out_bases, lengths, queries, query_ids):
    layer_count, example_count, seq_len, width_local = hidden_states.shape
    hidden_local = up_grads.shape[3]
    rank_size = in_bases.shape[2]
    states = hidden_states.astype(jnp.float32)
    squares = jnp.sum(states * states, axis=3)
    power = lax.psum(squares, "tensor")
    scaled = (states * gains.astype(jnp.float32)[:, None, None, :]).astype(jnp.bfloat16)
    positions = jnp.arange(seq_len, dtype=jnp.int32)
    valid_mask = positions[None, :] < lengths[:, None]
    grad_rows = jnp.where(valid_mask[None, :, :, None], up_grads, jnp.zeros((), jnp.bfloat16))
    flat_in = scaled.reshape(layer_count, example_count * seq_len, width_local)
    flat_out = grad_rows.reshape(layer_count, example_count * seq_len, hidden_local)
    shard_in = in_bases.shape[1]
    shard_out = out_bases.shape[1]
    blocks = math.gcd(shard_in, shard_out)
    per_in = shard_in // blocks
    per_out = shard_out // blocks
    grouped_in = in_bases.reshape(layer_count, blocks, per_in * rank_size)
    grouped_out = out_bases.reshape(layer_count, blocks, per_out * rank_size)
    pieces = (
        lax.all_gather(grouped_in, "dp", axis=1, tiled=True),
        lax.all_gather(grouped_out, "dp", axis=1, tiled=True),
    )
    block_count = pieces[0].shape[1]
    rows_in = pieces[0].reshape(layer_count, block_count * per_in, rank_size)
    rows_out = pieces[1].reshape(layer_count, block_count * per_out, rank_size)
    new_in = jnp.einsum("ltd,ldr->ltr", flat_in, rows_in, preferred_element_type=jnp.float32)
    new_out = jnp.einsum("ltd,ldr->ltr", flat_out, rows_out, preferred_element_type=jnp.float32)
    proj_in = new_in
    proj_out = new_out
    proj_in, proj_out = lax.psum((proj_in, proj_out), "tensor")
    full_width = width_local * lax.axis_size("tensor")
    inverse = lax.rsqrt(power / full_width + EPSILON)
    proj_in = proj_in * inverse.reshape(layer_count, example_count * seq_len)[:, :, None]
    kronecker = jnp.einsum(
        "lesi,lesj->elij",
        proj_in.reshape(layer_count, example_count, seq_len, rank_size),
        proj_out.reshape(layer_count, example_count, seq_len, rank_size),
    )
    example_grads = (
        (kronecker * seq_len ** (-0.5))
        .reshape(example_count, layer_count, rank_size * rank_size)
        .astype(jnp.bfloat16)
    )
    flat_grads = example_grads.reshape(example_count, layer_count * rank_size * rank_size)
    in_piece = lax.all_gather(queries, "dp", axis=0, tiled=True)
    all_scores = jnp.einsum(
        "ek,qk->eq",
        flat_grads,
        in_piece.reshape(in_piece.shape[0], -1),
        preferred_element_type=jnp.float32,
    )
    scores = jnp.take(all_scores, query_ids, axis=1)
    return (example_grads, scores)

WAYS = ("NMT", "MMT", "MNT")
TILES = (6, 6, 6)
LAG, LATE, ASK = 3, 5, 3


def remote(src, dst, send_sem, recv_sem, where):
    return pltpu.make_async_remote_copy(
        src_ref=src,
        dst_ref=dst,
        send_sem=send_sem,
        recv_sem=recv_sem,
        device_id=where,
        device_id_type=pl.DeviceIdType.MESH,
    )


def kernel(
    planes,
    widths,
    ways,
    lag,
    late,
    ask,
    hidden_ref,
    grads_ref,
    gains_hbm,
    in_ref,
    out_ref,
    lengths_hbm,
    queries_ref,
    ids_hbm,
    packed_ref,
    bases,
    hidden,
    scaled,
    grads,
    sum_in,
    sum_out,
    power,
    peer_power,
    mine,
    theirs,
    wide,
    all_queries,
    gains_ref,
    lengths_ref,
    ids_ref,
    local_sem,
    z_send,
    z_recv,
    x_send,
    x_recv,
    y_send,
    y_recv,
    x2_send,
    x2_recv,
    y2_send,
    y2_recv,
    q_send,
    q_recv,
    t_send,
    t_recv,
):
    group, dp, tensor = lax.axis_index("group"), lax.axis_index("dp"), lax.axis_index("tensor")
    z, x, y = dp // 2, dp % 2, group
    count = 2 * planes
    x_peer, y_peer, t_peer = {"dp": 2 * z + 1 - x}, {"group": 1 - y}, {"tensor": 1 - tensor}
    rank, wide_in, wide_out = in_ref.shape[0], in_ref.shape[1], out_ref.shape[1]
    half, quarter = rank // 2, rank // 4
    chunks = len(widths)
    edges = [sum(widths[:c]) for c in range(chunks + 1)]
    seq = hidden.shape[0]

    own_in = pltpu.make_async_copy(in_ref, bases.at[dp, :, pl.ds(0, wide_in)], local_sem.at[0])
    own_out = pltpu.make_async_copy(out_ref, bases.at[dp, :, pl.ds(wide_in, wide_out)], local_sem.at[1])
    own_hidden = pltpu.make_async_copy(hidden_ref, hidden, local_sem.at[2])
    own_grads = pltpu.make_async_copy(grads_ref, grads, local_sem.at[3])
    own_queries = pltpu.make_async_copy(queries_ref, all_queries.at[dp], local_sem.at[4])
    own_gains = pltpu.make_async_copy(gains_hbm, gains_ref, local_sem.at[5])
    own_lengths = pltpu.make_async_copy(lengths_hbm, lengths_ref, local_sem.at[6])
    own_ids = pltpu.make_async_copy(ids_hbm, ids_ref, local_sem.at[7])
    own_in.start()
    own_out.start()
    own_gains.start()
    own_queries.start()
    own_lengths.start()
    own_ids.start()
    own_hidden.start()
    own_grads.start()

    barrier = pltpu.get_barrier_semaphore()
    for step in range(1, count):
        pl.semaphore_signal(barrier, inc=1, device_id={"dp": (dp + step) % count}, device_id_type=pl.DeviceIdType.MESH)
    pl.semaphore_signal(barrier, inc=1, device_id=y_peer, device_id_type=pl.DeviceIdType.MESH)
    pl.semaphore_signal(barrier, inc=1, device_id=t_peer, device_id_type=pl.DeviceIdType.MESH)
    own_in.wait()
    own_out.wait()
    own_queries.wait()
    pl.semaphore_wait(barrier, count + 1)

    def rows(start, size):
        return pl.ds(pl.multiple_of(start, quarter), size)

    def columns(chunk):
        return pl.ds(edges[chunk], widths[chunk])

    def shard(plane, column, chunk):
        return bases.at[2 * plane + column, :, columns(chunk)]

    def part(plane, column, side, chunk):
        return bases.at[2 * plane + column, rows(half * side, half), columns(chunk)]

    def fourth(plane, column, side, which, chunk):
        return bases.at[2 * plane + column, rows(half * side + quarter * which, quarter), columns(chunk)]

    def along_z(plane, up, c, whole):
        there = {"dp": dp + 2} if up else {"dp": dp - 2}
        ref = shard(plane, x, c) if whole else part(plane, x, y, c)
        return remote(ref, ref, z_send.at[int(up), plane, c], z_recv.at[plane, c], there)

    def over_x(plane, column, c, whole=False):
        ref = shard(plane, column, c) if whole else part(plane, column, y, c)
        return remote(ref, ref, x_send.at[plane, c], x_recv.at[plane, c], x_peer)

    def over_y(plane, column, side, c):
        ref = part(plane, column, side, c)
        return remote(ref, ref, y_send.at[plane, c], y_recv.at[plane, c], y_peer)

    def second_x(plane, column, side, c):
        ref = fourth(plane, column, side, 0, c)
        return remote(ref, ref, x2_send.at[plane, c], x2_recv.at[plane, c], x_peer)

    def second_y(plane, column, side, c, way):
        ref = fourth(plane, column, side, 1, c) if way == "N" else part(plane, column, side, c)
        return remote(ref, ref, y2_send.at[plane, c], y2_recv.at[plane, c], y_peer)

    def to_query(step):
        there = (dp + step) % count
        return remote(all_queries.at[dp], all_queries.at[dp], q_send.at[step - 1], q_recv.at[dp], {"dp": there})

    def multiply(unit, chunk):
        contract = (((1,), (1,)), ((), ()))
        low, high = edges[chunk], edges[chunk + 1]
        for into, values, start, size in ((sum_in, scaled, 0, wide_in), (sum_out, grads, wide_in, wide_out)):
            first, last = max(low, start), min(high, start + size)
            if first < last:
                at = pl.ds(pl.multiple_of(unit * size + (first - start), 128), last - first)
                into[...] += lax.dot_general(
                    values[:, at], bases[unit, :, first:last], contract, preferred_element_type=jnp.float32
                )

    remote_planes = [(step, up) for step in range(1, planes) for up in (True, False)]

    def place(step, up):
        plane = z - step if up else z + step
        return plane, (plane >= 0) if up else (plane < planes)

    def onward(up):
        return (z < planes - 1) if up else (z > 0)

    def on_z(plane, step, up, c, do):
        takers = [far for far in range(step, planes) if ways[far - 1][c] in "FT"]
        if not takers or takers[0] == step:
            do(along_z(plane, up, c, bool(takers)))
            return
        last = (plane + takers[0] < planes) if up else (plane >= takers[0])

        @pl.when(last)
        def _():
            do(along_z(plane, up, c, True))

        @pl.when(jnp.logical_not(last))
        def _():
            do(along_z(plane, up, c, False))

    def own_sends(c, do):
        for up in (True, False):

            @pl.when(onward(up))
            def _(up=up):
                on_z(z, 1, up, c, do)

        do(over_x(z, x, c))

    def first_sends(plane, step, up, c, do):
        way = ways[step - 1][c]
        if step < planes - 1:

            @pl.when(onward(up))
            def _():
                on_z(plane, step + 1, up, c, do)

        do(over_x(plane, x, c, way == "T"))
        if way in "NM":
            do(over_y(plane, x, y, c))

    def begin(copy):
        copy.start()

    def arrived(copy):
        copy.wait_recv()

    def sent(copy):
        copy.wait_send()

    for c in range(chunks):
        own_sends(c, begin)

    own_gains.wait()
    own_hidden.wait()
    total = jnp.zeros((seq, 128), jnp.float32)
    for start in range(0, hidden.shape[1], 128):
        states = hidden[:, start : start + 128].astype(jnp.float32)
        total += states * states
        gain = gains_ref[:, start : start + 128].astype(jnp.float32)
        scaled[:, start : start + 128] = (states * gain).astype(jnp.bfloat16)
    power[...] = jnp.broadcast_to(jnp.sum(total, axis=1, keepdims=True), (seq, 128))
    send_power = remote(power, peer_power, t_send.at[0], t_recv.at[0], t_peer)
    send_power.start()
    sum_in[...] = jnp.zeros_like(sum_in)
    sum_out[...] = jnp.zeros_like(sum_out)
    own_grads.wait()
    for c in range(chunks):
        multiply(dp, c)

    def first_hop(step, up, c):
        plane, there = place(step, up)

        @pl.when(there)
        def _():
            on_z(plane, step, up, c, arrived)
            first_sends(plane, step, up, c, begin)

    def second_hop(step, up, c):
        plane, there = place(step, up)
        way = ways[step - 1][c]

        @pl.when(there)
        def _():
            over_x(plane, 1 - x, c, way == "T").wait_recv()
            if way in "NM":
                second_y(plane, 1 - x, y, c, way).start()
                over_y(plane, x, 1 - y, c).wait_recv()
            if way == "N":
                second_x(plane, x, 1 - y, c).start()
            if way == "F":
                over_y(plane, 1 - x, y, c).start()
            multiply(2 * plane + x, c)

    def finish(step, up, c):
        plane, there = place(step, up)
        way = ways[step - 1][c]

        @pl.when(there)
        def _():
            if way == "N":
                second_x(plane, 1 - x, 1 - y, c).wait_recv()
            if way in "NM":
                second_y(plane, 1 - x, 1 - y, c, way).wait_recv()
            if way == "F":
                over_y(plane, 1 - x, 1 - y, c).wait_recv()
            multiply(2 * plane + 1 - x, c)

    def all_sent(step, up, c):
        plane, there = place(step, up)
        way = ways[step - 1][c]

        @pl.when(there)
        def _():
            first_sends(plane, step, up, c, sent)
            if way in "NM":
                second_y(plane, 1 - x, y, c, way).wait_send()
            if way == "N":
                second_x(plane, x, 1 - y, c).wait_send()
            if way == "F":
                over_y(plane, 1 - x, y, c).wait_send()

    slots = (planes - 1) * chunks
    for slot in range(slots + lag + late):
        if slot < slots:
            for up in (True, False):
                first_hop(slot // chunks + 1, up, slot % chunks)
        if slot == ask:
            for other in range(1, count):
                to_query(other).start()
        again = slot - lag
        if -chunks <= again < 0:
            over_x(z, 1 - x, again + chunks).wait_recv()
            over_y(z, 1 - x, y, again + chunks).start()
        elif 0 <= again < slots:
            for up in (True, False):
                second_hop(again // chunks + 1, up, again % chunks)
        last = slot - lag - late
        if -chunks <= last < 0:
            over_y(z, 1 - x, 1 - y, last + chunks).wait_recv()
            multiply(2 * z + 1 - x, last + chunks)
        elif 0 <= last < slots:
            for up in (True, False):
                finish(last // chunks + 1, up, last % chunks)
        done = last - 1
        if -chunks <= done < 0:
            own_sends(done + chunks, sent)
            over_y(z, 1 - x, y, done + chunks).wait_send()
        elif 0 <= done < slots - late:
            for up in (True, False):
                all_sent(done // chunks + 1, up, done % chunks)

    mine[0] = sum_in[...]
    mine[1] = sum_out[...]
    send_sums = remote(mine, theirs, t_send.at[1], t_recv.at[1], t_peer)
    send_sums.start()
    for done in range(slots - late, slots):
        for up in (True, False):
            all_sent(done // chunks + 1, up, done % chunks)
    send_power.wait()
    mean = (power[...] + peer_power[...]) / (2 * hidden.shape[1])
    inverse = lax.rsqrt(mean + EPSILON)[:, :rank]
    own_lengths.wait()
    own_ids.wait()
    valid = lax.broadcasted_iota(jnp.int32, (seq, rank), 0) < lengths_ref[0]
    for other in range(1, count):
        remote(
            all_queries.at[dp], all_queries.at[(dp + other) % count], q_send.at[other - 1], q_recv.at[(dp + other) % count], x_peer
        ).wait_recv()
    for other in range(1, count):
        to_query(other).wait_send()
    send_sums.wait_recv()
    proj_in = ((mine[0] + theirs[0]) * inverse).astype(jnp.bfloat16)
    proj_out = jnp.where(valid, mine[1] + theirs[1], 0.0).astype(jnp.bfloat16)
    wide[...] = lax.dot_general(
        proj_in,
        jnp.concatenate([proj_out, proj_out], axis=1),
        (((0,), (0,)), ((), ())),
        preferred_element_type=jnp.float32,
    )
    even = wide[pl.ds(0, half, stride=2), :]
    odd = wide[pl.ds(1, half, stride=2), :]
    lane = lax.broadcasted_iota(jnp.int32, (half, 2 * rank), 1)
    flat = (jnp.where(lane < rank, even, odd) * seq ** (-0.5)).astype(jnp.bfloat16)
    flat = flat.astype(jnp.float32)
    packed_ref[:half, :] = flat
    per_device = all_queries.shape[1]
    score = jnp.zeros((count, per_device, 128), jnp.float32)
    for row in range(half):
        block = all_queries[:, :, row * 128 : (row + 1) * 128].astype(jnp.float32)
        score += block * flat[row : row + 1, :][None]
    score = jnp.sum(score, axis=2, keepdims=True)
    places = ids_ref.shape[1]
    number = per_device * lax.broadcasted_iota(jnp.int32, (count, per_device, places), 0) + lax.broadcasted_iota(
        jnp.int32, (count, per_device, places), 1
    )
    picked = jnp.where(number == ids_ref[...][None], score, 0.0)
    packed_ref[half : half + 1, :places] = jnp.sum(jnp.sum(picked, axis=0), axis=0, keepdims=True)

    send_sums.wait_send()


def lay_out(packed_ref, grads_ref, scores_ref):
    lines = grads_ref.shape[2] // 128
    for line in range(lines):
        grads_ref[0, :, line * 128 : (line + 1) * 128] = packed_ref[line : line + 1, :].astype(jnp.bfloat16)
    scores_ref[...] = packed_ref[lines : lines + 1, : scores_ref.shape[1]]


def local(hidden_states, up_grads, gains, in_bases, out_bases, lengths, queries, query_ids):
    layer_count, example_count, seq, width = hidden_states.shape
    hidden_units = up_grads.shape[3]
    shard_in, rank = in_bases.shape[1:]
    shard_out = out_bases.shape[1]
    count = lax.axis_size("dp")
    fits = (
        (layer_count, example_count, rank, lax.axis_size("group"), lax.axis_size("tensor")) == (1, 1, 64, 2, 2)
        and count % 2 == 0
        and shard_in % 128 == 0
        and shard_out % 128 == 0
    )
    if not fits:
        return gathered_local(hidden_states, up_grads, gains, in_bases, out_bases, lengths, queries, query_ids)
    planes = count // 2
    tiles = (shard_in + shard_out) // 128
    fitted = planes - 1 == len(WAYS) and tiles == sum(TILES)
    widths = tuple(128 * tile for tile in TILES) if fitted else (128 * tiles,)
    chunks = len(widths)
    ways = WAYS if fitted else ("N",) * (planes - 1)
    lag, late, ask = (LAG, LATE, ASK) if fitted else (1, 1, 1)
    hbm, vmem = pl.BlockSpec(memory_space=pltpu.HBM), pl.BlockSpec(memory_space=pltpu.VMEM)
    pairs = pltpu.SemaphoreType.DMA((planes, chunks))
    f32, bf16 = jnp.float32, jnp.bfloat16
    packed = pl.pallas_call(
        functools.partial(kernel, planes, widths, ways, lag, late, ask),
        out_shape=jax.ShapeDtypeStruct((rank // 2 + 8, 2 * rank), f32),
        in_specs=[hbm] * 8,
        out_specs=vmem,
        scratch_shapes=[
            pltpu.VMEM((count, rank, shard_in + shard_out), bf16),
            pltpu.VMEM((seq, width), bf16),
            pltpu.VMEM((seq, width), bf16),
            pltpu.VMEM((seq, hidden_units), bf16),
            pltpu.VMEM((seq, rank), f32),
            pltpu.VMEM((seq, rank), f32),
            pltpu.VMEM((seq, 128), f32),
            pltpu.VMEM((seq, 128), f32),
            pltpu.VMEM((2, seq, rank), f32),
            pltpu.VMEM((2, seq, rank), f32),
            pltpu.VMEM((rank, 2 * rank), f32),
            pltpu.VMEM((count, queries.shape[0], rank * rank), bf16),
            pltpu.VMEM((1, width), bf16),
            pltpu.SMEM(lengths.shape, jnp.int32),
            pltpu.VMEM((1, query_ids.shape[0]), jnp.int32),
            pltpu.SemaphoreType.DMA((8,)),
            pltpu.SemaphoreType.DMA((2, planes, chunks)),
            pairs,
            pairs,
            pairs,
            pairs,
            pairs,
            pairs,
            pairs,
            pairs,
            pairs,
            pltpu.SemaphoreType.DMA((count - 1,)),
            pltpu.SemaphoreType.DMA((count,)),
            pltpu.SemaphoreType.DMA((2,)),
            pltpu.SemaphoreType.DMA((2,)),
        ],
        compiler_params=pltpu.CompilerParams(
            collective_id=0, has_side_effects=True, vmem_limit_bytes=64 * 1024 * 1024
        ),
    )(
        hidden_states.reshape(seq, width),
        up_grads.reshape(seq, hidden_units),
        gains,
        in_bases[0].T,
        out_bases[0].T,
        lengths,
        queries.reshape(queries.shape[0], -1),
        query_ids.reshape(1, -1),
    )
    return pl.pallas_call(
        lay_out,
        out_shape=(
            jax.ShapeDtypeStruct((1, 1, rank * rank), bf16),
            jax.ShapeDtypeStruct((1, query_ids.shape[0]), f32),
        ),
        in_specs=[vmem],
        out_specs=(vmem, vmem),
    )(packed)


def solution(mesh):
    placed = (
        P(None, ("group", "dp"), None, "tensor"),
        P(None, ("group", "dp"), None, "tensor"),
        P(None, "tensor"),
        P(None, ("tensor", "dp"), None),
        P(None, ("tensor", "dp"), None),
        P(("group", "dp")),
        P(("group", "dp"), None, None),
        P("group"),
    )
    return jax.shard_map(
        local,
        mesh=mesh,
        in_specs=placed,
        out_specs=(P(("group", "dp"), None, None), P(("group", "dp"), None)),
        check_vma=False,
    )
```

```python
import functools
import math

import jax
import jax.numpy as jnp
from jax import lax
from jax.experimental import pallas as pl
from jax.experimental.pallas import tpu as pltpu
from jax.sharding import PartitionSpec as P

EPSILON = 1e-05


def gathered_local(hidden_states, up_grads, gains, in_bases, out_bases, lengths, queries, query_ids):
    layer_count, example_count, seq_len, width_local = hidden_states.shape
    hidden_local = up_grads.shape[3]
    rank_size = in_bases.shape[2]
    states = hidden_states.astype(jnp.float32)
    squares = jnp.sum(states * states, axis=3)
    power = lax.psum(squares, "tensor")
    scaled = (states * gains.astype(jnp.float32)[:, None, None, :]).astype(jnp.bfloat16)
    positions = jnp.arange(seq_len, dtype=jnp.int32)
    valid_mask = positions[None, :] < lengths[:, None]
    grad_rows = jnp.where(valid_mask[None, :, :, None], up_grads, jnp.zeros((), jnp.bfloat16))
    flat_in = scaled.reshape(layer_count, example_count * seq_len, width_local)
    flat_out = grad_rows.reshape(layer_count, example_count * seq_len, hidden_local)
    shard_in = in_bases.shape[1]
    shard_out = out_bases.shape[1]
    blocks = math.gcd(shard_in, shard_out)
    per_in = shard_in // blocks
    per_out = shard_out // blocks
    grouped_in = in_bases.reshape(layer_count, blocks, per_in * rank_size)
    grouped_out = out_bases.reshape(layer_count, blocks, per_out * rank_size)
    pieces = (
        lax.all_gather(grouped_in, "dp", axis=1, tiled=True),
        lax.all_gather(grouped_out, "dp", axis=1, tiled=True),
    )
    block_count = pieces[0].shape[1]
    rows_in = pieces[0].reshape(layer_count, block_count * per_in, rank_size)
    rows_out = pieces[1].reshape(layer_count, block_count * per_out, rank_size)
    new_in = jnp.einsum("ltd,ldr->ltr", flat_in, rows_in, preferred_element_type=jnp.float32)
    new_out = jnp.einsum("ltd,ldr->ltr", flat_out, rows_out, preferred_element_type=jnp.float32)
    proj_in = new_in
    proj_out = new_out
    proj_in, proj_out = lax.psum((proj_in, proj_out), "tensor")
    full_width = width_local * lax.axis_size("tensor")
    inverse = lax.rsqrt(power / full_width + EPSILON)
    proj_in = proj_in * inverse.reshape(layer_count, example_count * seq_len)[:, :, None]
    kronecker = jnp.einsum(
        "lesi,lesj->elij",
        proj_in.reshape(layer_count, example_count, seq_len, rank_size),
        proj_out.reshape(layer_count, example_count, seq_len, rank_size),
    )
    example_grads = (
        (kronecker * seq_len ** (-0.5))
        .reshape(example_count, layer_count, rank_size * rank_size)
        .astype(jnp.bfloat16)
    )
    flat_grads = example_grads.reshape(example_count, layer_count * rank_size * rank_size)
    in_piece = lax.all_gather(queries, "dp", axis=0, tiled=True)
    all_scores = jnp.einsum(
        "ek,qk->eq",
        flat_grads,
        in_piece.reshape(in_piece.shape[0], -1),
        preferred_element_type=jnp.float32,
    )
    scores = jnp.take(all_scores, query_ids, axis=1)
    return (example_grads, scores)

WAYS = ("NMT", "MMT", "MNT")
TILES = (7, 5, 6)
LAG, LATE, ASK = 3, 5, 3


def remote(src, dst, send_sem, recv_sem, where):
    return pltpu.make_async_remote_copy(
        src_ref=src,
        dst_ref=dst,
        send_sem=send_sem,
        recv_sem=recv_sem,
        device_id=where,
        device_id_type=pl.DeviceIdType.MESH,
    )


def kernel(
    planes,
    widths,
    ways,
    lag,
    late,
    ask,
    hidden_ref,
    grads_ref,
    gains_hbm,
    in_ref,
    out_ref,
    lengths_hbm,
    queries_ref,
    ids_hbm,
    packed_ref,
    bases,
    hidden,
    scaled,
    grads,
    sum_in,
    sum_out,
    power,
    peer_power,
    mine,
    theirs,
    wide,
    all_queries,
    gains_ref,
    lengths_ref,
    ids_ref,
    local_sem,
    z_send,
    z_recv,
    x_send,
    x_recv,
    y_send,
    y_recv,
    x2_send,
    x2_recv,
    y2_send,
    y2_recv,
    q_send,
    q_recv,
    t_send,
    t_recv,
):
    group, dp, tensor = lax.axis_index("group"), lax.axis_index("dp"), lax.axis_index("tensor")
    z, x, y = dp // 2, dp % 2, group
    count = 2 * planes
    x_peer, y_peer, t_peer = {"dp": 2 * z + 1 - x}, {"group": 1 - y}, {"tensor": 1 - tensor}
    rank, wide_in, wide_out = in_ref.shape[0], in_ref.shape[1], out_ref.shape[1]
    half, quarter = rank // 2, rank // 4
    chunks = len(widths)
    edges = [sum(widths[:c]) for c in range(chunks + 1)]
    seq = hidden.shape[0]

    own_in = pltpu.make_async_copy(in_ref, bases.at[dp, :, pl.ds(0, wide_in)], local_sem.at[0])
    own_out = pltpu.make_async_copy(out_ref, bases.at[dp, :, pl.ds(wide_in, wide_out)], local_sem.at[1])
    own_hidden = pltpu.make_async_copy(hidden_ref, hidden, local_sem.at[2])
    own_grads = pltpu.make_async_copy(grads_ref, grads, local_sem.at[3])
    own_queries = pltpu.make_async_copy(queries_ref, all_queries.at[dp], local_sem.at[4])
    own_gains = pltpu.make_async_copy(gains_hbm, gains_ref, local_sem.at[5])
    own_lengths = pltpu.make_async_copy(lengths_hbm, lengths_ref, local_sem.at[6])
    own_ids = pltpu.make_async_copy(ids_hbm, ids_ref, local_sem.at[7])
    own_in.start()
    own_out.start()
    own_gains.start()
    own_queries.start()
    own_lengths.start()
    own_ids.start()
    own_hidden.start()
    own_grads.start()

    barrier = pltpu.get_barrier_semaphore()
    for step in range(1, count):
        pl.semaphore_signal(barrier, inc=1, device_id={"dp": (dp + step) % count}, device_id_type=pl.DeviceIdType.MESH)
    pl.semaphore_signal(barrier, inc=1, device_id=y_peer, device_id_type=pl.DeviceIdType.MESH)
    pl.semaphore_signal(barrier, inc=1, device_id=t_peer, device_id_type=pl.DeviceIdType.MESH)
    own_in.wait()
    own_out.wait()
    own_queries.wait()
    pl.semaphore_wait(barrier, count + 1)

    def rows(start, size):
        return pl.ds(pl.multiple_of(start, quarter), size)

    def columns(chunk):
        return pl.ds(edges[chunk], widths[chunk])

    def shard(plane, column, chunk):
        return bases.at[2 * plane + column, :, columns(chunk)]

    def part(plane, column, side, chunk):
        return bases.at[2 * plane + column, rows(half * side, half), columns(chunk)]

    def fourth(plane, column, side, which, chunk):
        return bases.at[2 * plane + column, rows(half * side + quarter * which, quarter), columns(chunk)]

    def along_z(plane, up, c, whole):
        there = {"dp": dp + 2} if up else {"dp": dp - 2}
        ref = shard(plane, x, c) if whole else part(plane, x, y, c)
        return remote(ref, ref, z_send.at[int(up), plane, c], z_recv.at[plane, c], there)

    def over_x(plane, column, c, whole=False):
        ref = shard(plane, column, c) if whole else part(plane, column, y, c)
        return remote(ref, ref, x_send.at[plane, c], x_recv.at[plane, c], x_peer)

    def over_y(plane, column, side, c):
        ref = part(plane, column, side, c)
        return remote(ref, ref, y_send.at[plane, c], y_recv.at[plane, c], y_peer)

    def second_x(plane, column, side, c):
        ref = fourth(plane, column, side, 0, c)
        return remote(ref, ref, x2_send.at[plane, c], x2_recv.at[plane, c], x_peer)

    def second_y(plane, column, side, c, way):
        ref = fourth(plane, column, side, 1, c) if way == "N" else part(plane, column, side, c)
        return remote(ref, ref, y2_send.at[plane, c], y2_recv.at[plane, c], y_peer)

    def to_query(step):
        there = (dp + step) % count
        return remote(all_queries.at[dp], all_queries.at[dp], q_send.at[step - 1], q_recv.at[dp], {"dp": there})

    def multiply(unit, chunk):
        contract = (((1,), (1,)), ((), ()))
        low, high = edges[chunk], edges[chunk + 1]
        for into, values, start, size in ((sum_in, scaled, 0, wide_in), (sum_out, grads, wide_in, wide_out)):
            first, last = max(low, start), min(high, start + size)
            if first < last:
                at = pl.ds(pl.multiple_of(unit * size + (first - start), 128), last - first)
                into[...] += lax.dot_general(
                    values[:, at], bases[unit, :, first:last], contract, preferred_element_type=jnp.float32
                )

    remote_planes = [(step, up) for step in range(1, planes) for up in (True, False)]

    def place(step, up):
        plane = z - step if up else z + step
        return plane, (plane >= 0) if up else (plane < planes)

    def onward(up):
        return (z < planes - 1) if up else (z > 0)

    def on_z(plane, step, up, c, do):
        takers = [far for far in range(step, planes) if ways[far - 1][c] in "FT"]
        if not takers or takers[0] == step:
            do(along_z(plane, up, c, bool(takers)))
            return
        last = (plane + takers[0] < planes) if up else (plane >= takers[0])

        @pl.when(last)
        def _():
            do(along_z(plane, up, c, True))

        @pl.when(jnp.logical_not(last))
        def _():
            do(along_z(plane, up, c, False))

    def own_sends(c, do):
        for up in (True, False):

            @pl.when(onward(up))
            def _(up=up):
                on_z(z, 1, up, c, do)

        do(over_x(z, x, c))

    def first_sends(plane, step, up, c, do):
        way = ways[step - 1][c]
        if step < planes - 1:

            @pl.when(onward(up))
            def _():
                on_z(plane, step + 1, up, c, do)

        do(over_x(plane, x, c, way == "T"))
        if way in "NM":
            do(over_y(plane, x, y, c))

    def begin(copy):
        copy.start()

    def arrived(copy):
        copy.wait_recv()

    def sent(copy):
        copy.wait_send()

    for c in range(chunks):
        own_sends(c, begin)

    own_gains.wait()
    own_hidden.wait()
    total = jnp.zeros((seq, 128), jnp.float32)
    for start in range(0, hidden.shape[1], 128):
        states = hidden[:, start : start + 128].astype(jnp.float32)
        total += states * states
        gain = gains_ref[:, start : start + 128].astype(jnp.float32)
        scaled[:, start : start + 128] = (states * gain).astype(jnp.bfloat16)
    power[...] = jnp.broadcast_to(jnp.sum(total, axis=1, keepdims=True), (seq, 128))
    send_power = remote(power, peer_power, t_send.at[0], t_recv.at[0], t_peer)
    send_power.start()
    sum_in[...] = jnp.zeros_like(sum_in)
    sum_out[...] = jnp.zeros_like(sum_out)
    own_grads.wait()
    for c in range(chunks):
        multiply(dp, c)

    def first_hop(step, up, c):
        plane, there = place(step, up)

        @pl.when(there)
        def _():
            on_z(plane, step, up, c, arrived)
            first_sends(plane, step, up, c, begin)

    def second_hop(step, up, c):
        plane, there = place(step, up)
        way = ways[step - 1][c]

        @pl.when(there)
        def _():
            over_x(plane, 1 - x, c, way == "T").wait_recv()
            if way in "NM":
                second_y(plane, 1 - x, y, c, way).start()
                over_y(plane, x, 1 - y, c).wait_recv()
            if way == "N":
                second_x(plane, x, 1 - y, c).start()
            if way == "F":
                over_y(plane, 1 - x, y, c).start()
            multiply(2 * plane + x, c)

    def finish(step, up, c):
        plane, there = place(step, up)
        way = ways[step - 1][c]

        @pl.when(there)
        def _():
            if way == "N":
                second_x(plane, 1 - x, 1 - y, c).wait_recv()
            if way in "NM":
                second_y(plane, 1 - x, 1 - y, c, way).wait_recv()
            if way == "F":
                over_y(plane, 1 - x, 1 - y, c).wait_recv()
            multiply(2 * plane + 1 - x, c)

    def all_sent(step, up, c):
        plane, there = place(step, up)
        way = ways[step - 1][c]

        @pl.when(there)
        def _():
            first_sends(plane, step, up, c, sent)
            if way in "NM":
                second_y(plane, 1 - x, y, c, way).wait_send()
            if way == "N":
                second_x(plane, x, 1 - y, c).wait_send()
            if way == "F":
                over_y(plane, 1 - x, y, c).wait_send()

    slots = (planes - 1) * chunks
    for slot in range(slots + lag + late):
        if slot < slots:
            for up in (True, False):
                first_hop(slot // chunks + 1, up, slot % chunks)
        if slot == ask:
            for other in range(1, count):
                to_query(other).start()
        again = slot - lag
        if -chunks <= again < 0:
            over_x(z, 1 - x, again + chunks).wait_recv()
            over_y(z, 1 - x, y, again + chunks).start()
        elif 0 <= again < slots:
            for up in (True, False):
                second_hop(again // chunks + 1, up, again % chunks)
        last = slot - lag - late
        if -chunks <= last < 0:
            over_y(z, 1 - x, 1 - y, last + chunks).wait_recv()
            multiply(2 * z + 1 - x, last + chunks)
        elif 0 <= last < slots:
            for up in (True, False):
                finish(last // chunks + 1, up, last % chunks)
        done = last - 1
        if -chunks <= done < 0:
            own_sends(done + chunks, sent)
            over_y(z, 1 - x, y, done + chunks).wait_send()
        elif 0 <= done < slots - late:
            for up in (True, False):
                all_sent(done // chunks + 1, up, done % chunks)

    mine[0] = sum_in[...]
    mine[1] = sum_out[...]
    send_sums = remote(mine, theirs, t_send.at[1], t_recv.at[1], t_peer)
    send_sums.start()
    for done in range(slots - late, slots):
        for up in (True, False):
            all_sent(done // chunks + 1, up, done % chunks)
    send_power.wait()
    mean = (power[...] + peer_power[...]) / (2 * hidden.shape[1])
    inverse = lax.rsqrt(mean + EPSILON)[:, :rank]
    own_lengths.wait()
    own_ids.wait()
    valid = lax.broadcasted_iota(jnp.int32, (seq, rank), 0) < lengths_ref[0]
    for other in range(1, count):
        remote(
            all_queries.at[dp], all_queries.at[(dp + other) % count], q_send.at[other - 1], q_recv.at[(dp + other) % count], x_peer
        ).wait_recv()
    for other in range(1, count):
        to_query(other).wait_send()
    send_sums.wait_recv()
    proj_in = ((mine[0] + theirs[0]) * inverse).astype(jnp.bfloat16)
    proj_out = jnp.where(valid, mine[1] + theirs[1], 0.0).astype(jnp.bfloat16)
    wide[...] = lax.dot_general(
        proj_in,
        jnp.concatenate([proj_out, proj_out], axis=1),
        (((0,), (0,)), ((), ())),
        preferred_element_type=jnp.float32,
    )
    even = wide[pl.ds(0, half, stride=2), :]
    odd = wide[pl.ds(1, half, stride=2), :]
    lane = lax.broadcasted_iota(jnp.int32, (half, 2 * rank), 1)
    flat = (jnp.where(lane < rank, even, odd) * seq ** (-0.5)).astype(jnp.bfloat16)
    flat = flat.astype(jnp.float32)
    packed_ref[:half, :] = flat
    per_device = all_queries.shape[1]
    score = jnp.zeros((count, per_device, 128), jnp.float32)
    for row in range(half):
        block = all_queries[:, :, row * 128 : (row + 1) * 128].astype(jnp.float32)
        score += block * flat[row : row + 1, :][None]
    score = jnp.sum(score, axis=2, keepdims=True)
    places = ids_ref.shape[1]
    number = per_device * lax.broadcasted_iota(jnp.int32, (count, per_device, places), 0) + lax.broadcasted_iota(
        jnp.int32, (count, per_device, places), 1
    )
    picked = jnp.where(number == ids_ref[...][None], score, 0.0)
    packed_ref[half : half + 1, :places] = jnp.sum(jnp.sum(picked, axis=0), axis=0, keepdims=True)

    send_sums.wait_send()


def lay_out(packed_ref, grads_ref, scores_ref):
    lines = grads_ref.shape[2] // 128
    for line in range(lines):
        grads_ref[0, :, line * 128 : (line + 1) * 128] = packed_ref[line : line + 1, :].astype(jnp.bfloat16)
    scores_ref[...] = packed_ref[lines : lines + 1, : scores_ref.shape[1]]


def local(hidden_states, up_grads, gains, in_bases, out_bases, lengths, queries, query_ids):
    layer_count, example_count, seq, width = hidden_states.shape
    hidden_units = up_grads.shape[3]
    shard_in, rank = in_bases.shape[1:]
    shard_out = out_bases.shape[1]
    count = lax.axis_size("dp")
    fits = (
        (layer_count, example_count, rank, lax.axis_size("group"), lax.axis_size("tensor")) == (1, 1, 64, 2, 2)
        and count % 2 == 0
        and shard_in % 128 == 0
        and shard_out % 128 == 0
    )
    if not fits:
        return gathered_local(hidden_states, up_grads, gains, in_bases, out_bases, lengths, queries, query_ids)
    planes = count // 2
    tiles = (shard_in + shard_out) // 128
    fitted = planes - 1 == len(WAYS) and tiles == sum(TILES)
    widths = tuple(128 * tile for tile in TILES) if fitted else (128 * tiles,)
    chunks = len(widths)
    ways = WAYS if fitted else ("N",) * (planes - 1)
    lag, late, ask = (LAG, LATE, ASK) if fitted else (1, 1, 1)
    hbm, vmem = pl.BlockSpec(memory_space=pltpu.HBM), pl.BlockSpec(memory_space=pltpu.VMEM)
    pairs = pltpu.SemaphoreType.DMA((planes, chunks))
    f32, bf16 = jnp.float32, jnp.bfloat16
    packed = pl.pallas_call(
        functools.partial(kernel, planes, widths, ways, lag, late, ask),
        out_shape=jax.ShapeDtypeStruct((rank // 2 + 8, 2 * rank), f32),
        in_specs=[hbm] * 8,
        out_specs=vmem,
        scratch_shapes=[
            pltpu.VMEM((count, rank, shard_in + shard_out), bf16),
            pltpu.VMEM((seq, width), bf16),
            pltpu.VMEM((seq, width), bf16),
            pltpu.VMEM((seq, hidden_units), bf16),
            pltpu.VMEM((seq, rank), f32),
            pltpu.VMEM((seq, rank), f32),
            pltpu.VMEM((seq, 128), f32),
            pltpu.VMEM((seq, 128), f32),
            pltpu.VMEM((2, seq, rank), f32),
            pltpu.VMEM((2, seq, rank), f32),
            pltpu.VMEM((rank, 2 * rank), f32),
            pltpu.VMEM((count, queries.shape[0], rank * rank), bf16),
            pltpu.VMEM((1, width), bf16),
            pltpu.SMEM(lengths.shape, jnp.int32),
            pltpu.VMEM((1, query_ids.shape[0]), jnp.int32),
            pltpu.SemaphoreType.DMA((8,)),
            pltpu.SemaphoreType.DMA((2, planes, chunks)),
            pairs,
            pairs,
            pairs,
            pairs,
            pairs,
            pairs,
            pairs,
            pairs,
            pairs,
            pltpu.SemaphoreType.DMA((count - 1,)),
            pltpu.SemaphoreType.DMA((count,)),
            pltpu.SemaphoreType.DMA((2,)),
            pltpu.SemaphoreType.DMA((2,)),
        ],
        compiler_params=pltpu.CompilerParams(
            collective_id=0, has_side_effects=True, vmem_limit_bytes=64 * 1024 * 1024
        ),
    )(
        hidden_states.reshape(seq, width),
        up_grads.reshape(seq, hidden_units),
        gains,
        in_bases[0].T,
        out_bases[0].T,
        lengths,
        queries.reshape(queries.shape[0], -1),
        query_ids.reshape(1, -1),
    )
    return pl.pallas_call(
        lay_out,
        out_shape=(
            jax.ShapeDtypeStruct((1, 1, rank * rank), bf16),
            jax.ShapeDtypeStruct((1, query_ids.shape[0]), f32),
        ),
        in_specs=[vmem],
        out_specs=(vmem, vmem),
    )(packed)


def solution(mesh):
    placed = (
        P(None, ("group", "dp"), None, "tensor"),
        P(None, ("group", "dp"), None, "tensor"),
        P(None, "tensor"),
        P(None, ("tensor", "dp"), None),
        P(None, ("tensor", "dp"), None),
        P(("group", "dp")),
        P(("group", "dp"), None, None),
        P("group"),
    )
    return jax.shard_map(
        local,
        mesh=mesh,
        in_specs=placed,
        out_specs=(P(("group", "dp"), None, None), P(("group", "dp"), None)),
        check_vma=False,
    )
```
